256 devices in a mesh: gx: 16 (over z_hi, y), gy: 16 (over z_lo, x, core).
Axes of the slice: x: 4, y: 4, z: 8 (z_hi: 4, z_lo: 2; z = z_hi * 2 + z_lo), core: 2. Of those that a mesh axis runs over, the one named last changes fastest.
Arguments:
- snapshot: float32 [8, 512, 512, 128], P(None, 'gx', 'gy'), may hold values from -20 to 20
- start_factor: float32 [512, 128], replicated, may hold values from -0.25 to 0.25
Outputs:
- factor: float32 [512, 128], replicated
- core: float32 [128, 8, 512, 128], P('gx', None, 'gy')
The draws below stay inside these ranges and needn't reach their ends.
All inputs are finite; a program needn't handle non-finite values.
Results may differ from the reference program's by a relative error of at most 0.00018.
Values sent between devices are 32-bit elements; how exact they have to be, the bound alone decides.
A program may use at most 64 MiB of HBM per device.

```python
import math
import jax
import jax.numpy as jnp
from jax import lax

V = 8
N1 = 512
RANK = 128
N3 = 128
ITERS = 2
N2 = 512


def draw_snapshot(key, part):
    key = jax.random.fold_in(key, 11)
    key_rows, key_cells = jax.random.split(key)
    scales = jnp.exp(jax.random.uniform(key_rows, (1, N1, 1, 1), jnp.float32) * math.log(3.0))
    cells = jnp.clip(jax.random.normal(key_cells, (V, N1, N2, N3), jnp.float32), -5.0, 5.0)
    return (scales * cells).astype(jnp.float32)


def noise(stream_key, dims, width, limit, kind=jnp.bfloat16):
    array = width * jax.random.normal(stream_key, dims, jnp.float32)
    return jnp.clip(array, min=-limit, max=limit).astype(kind)


def setup_inputs(seed: int = 0) -> dict:
    key_of = jax.random.split(jax.random.key(seed), 3)
    snapshot = draw_snapshot(jax.random.fold_in(key_of[2], 71), 0)
    start_factor = noise(key_of[1], (N1, RANK), N1 ** -0.5, 0.25, jnp.float32)
    return {"snapshot": snapshot, "start_factor": start_factor}


def reference(snapshot, start_factor):
    gram = jnp.einsum('vabc,vdbc->ad', snapshot, snapshot, precision=lax.Precision.HIGHEST)
    basis = start_factor
    for step in range(ITERS):
        image = jnp.dot(gram, basis, precision=lax.Precision.HIGHEST)
        small = jnp.dot(image.T, image, precision=lax.Precision.HIGHEST)
        lower = jnp.linalg.cholesky(small)
        basis = jax.scipy.linalg.solve_triangular(lower, image.T, lower=True).T
    factor = basis * math.sqrt(N1)
    core = jnp.einsum('ar,vabc->rvbc', basis, snapshot, precision=lax.Precision.HIGHEST)
    return (factor, core)
```

```python
import functools
import math

import jax
import jax.numpy as jnp
from jax import lax
from jax.experimental import pallas as pl
from jax.experimental.pallas import tpu as pltpu
from jax.sharding import PartitionSpec as P

ITERS = 2
MESH = pl.DeviceIdType.MESH
HIGHEST = lax.Precision.HIGHEST
F32, BF16 = jnp.float32, jnp.bfloat16

GX_OFFSETS = [(dz, dy) for dz in range(4) for dy in range(4) if dz or dy]
XY_OFFSETS = [(dx, dy) for dx in range(4) for dy in range(4) if dx or dy]
BLOCKS = [(i, j) for i in range(4) for j in range(i + 1)]
SLICE = 5


def dot(a, b, contract, precision=None):
    return lax.dot_general(a, b, ((contract[:1], contract[1:]), ((), ())), precision=precision, preferred_element_type=F32)


def split(x):
    hi = x.astype(BF16)
    return hi, (x - hi.astype(F32)).astype(BF16)


def dot3(a, b, contract):
    return dot(a[0], b[0], contract) + (dot(a[0], b[1], contract) + dot(a[1], b[0], contract))


def place():
    gx, gy = lax.axis_index("gx"), lax.axis_index("gy")
    return gx // 4, gx % 4, gy // 8, (gy // 2) % 4, gy % 2


def gx_peer(dz, dy):
    zh, y, _, _, _ = place()
    return lax.rem(zh + dz, 4) * 4 + lax.rem(y + dy, 4)


def xy_peer(dx, dy):
    zh, y, zl, x, c = place()
    x, y = lax.rem(x + dx, 4), lax.rem(y + dy, 4)
    return x * 4 + y, (zh * 4 + y, zl * 8 + x * 2 + c)


def z_peer(dz):
    zh, y, zl, x, c = place()
    z = lax.rem(zh * 2 + zl + dz, 8)
    return (z // 2 * 4 + y, z % 2 * 8 + x * 2 + c)


def core_peer():
    zh, y, zl, x, c = place()
    return (zh * 4 + y, zl * 8 + x * 2 + 1 - c)


def remote(src, dst, send, recv, device):
    return pltpu.make_async_remote_copy(src_ref=src, dst_ref=dst, send_sem=send, recv_sem=recv, device_id=device, device_id_type=MESH)


def gram_kernel(
    snap, gram, cells_out, cells, high, low, partial, core_buf, part, xy_buf, z_own, z_buf, done,
    local_sem, out_sem, send_sem, recv_sem, csend, crecv, xsend, xrecv, zsend, zrecv, gsend, grecv, fsend, frecv,
):
    gx, gy = lax.axis_index("gx"), lax.axis_index("gy")
    zh, y, zl, x, c = place()
    z = zh * 2 + zl
    barrier = pltpu.get_barrier_semaphore()
    for dz, dy in GX_OFFSETS:
        pl.semaphore_signal(barrier, inc=1, device_id=(gx_peer(dz, dy), gy), device_id_type=MESH)
    for dx, dy in XY_OFFSETS:
        if dx:
            pl.semaphore_signal(barrier, inc=1, device_id=xy_peer(dx, dy)[1], device_id_type=MESH)
    for dz in range(1, 8, 2):
        pl.semaphore_signal(barrier, inc=1, device_id=z_peer(dz), device_id_type=MESH)
    pl.semaphore_signal(barrier, inc=1, device_id=core_peer(), device_id_type=MESH)

    def source(home, h):
        return snap.at[home // 2, :, pl.ds(pl.multiple_of(home % 2 * 16 + h * 8, 8), 8), :]

    own_rows = pl.ds(pl.multiple_of(gx * 32, 32), 32)
    own = [pltpu.make_async_copy(source(gx, h), cells.at[h, own_rows], local_sem.at[h]) for h in range(2)]
    for copy in own:
        copy.start()
    pl.semaphore_wait(barrier, 15 + 12 + 4 + 1)
    moves = []
    for h in range(2):
        for n, (dz, dy) in enumerate(GX_OFFSETS):
            home = gx_peer(dz, dy)
            moves.append(remote(source(home, h), cells.at[h, own_rows], send_sem.at[h * 15 + n], recv_sem.at[h * 15 + n], (home, gy)))
            moves[-1].start()

    flat = cells.reshape(2 * 512 * 8, 128)
    for h in range(2):
        own[h].wait()
        for move in moves[h * 15 : h * 15 + 15]:
            move.wait_recv()
        for b in range(8):
            for q in range(4):
                rows = flat[pl.ds((h * 512 + q * 128) * 8 + b, 128, stride=8), :]
                hi, lo = split(rows)
                high[pl.ds(q * 128, 128), pl.ds(b * 128, 128)] = hi
                low[pl.ds(q * 128, 128), pl.ds(b * 128, 128)] = lo
        pltpu.make_async_copy(cells.at[h], cells_out.at[h], out_sem.at[h]).start()
        for first, start in ((0, 0), (2, 256)):
            rows, cols = pl.ds(start, 512 - start), pl.ds(start, 256)
            term = dot3((high[rows, :], low[rows, :]), (high[cols, :], low[cols, :]), (1, 1))
            for n, (i, j) in enumerate(BLOCKS):
                if j in (first, first + 1):
                    block = term[i * 128 - start : i * 128 - start + 128, (j - first) * 128 : (j - first) * 128 + 128]
                    if h:
                        block = block + partial[pl.ds(n * 128, 128), :]
                    partial[pl.ds(n * 128, 128), :] = block

    half = 80 * 8
    mine, other = pl.ds(pl.multiple_of(c * half, half), half), pl.ds(pl.multiple_of((1 - c) * half, half), half)
    swap = remote(partial.at[other], core_buf, csend.at[0], crecv.at[0], core_peer())
    swap.start()
    swap.wait_recv()
    part[...] = partial[mine, :] + core_buf[...]

    size = SLICE * 8
    me = x * 4 + y
    outs = []
    for n, (dx, dy) in enumerate(XY_OFFSETS):
        q, device = xy_peer(dx, dy)
        outs.append(remote(part.at[pl.ds(pl.multiple_of(q * size, size), size)], xy_buf.at[me], xsend.at[n], xrecv.at[n], device))
        outs[-1].start()
    xy_buf[me] = part[pl.ds(pl.multiple_of(me * size, size), size), :]
    for move in outs:
        move.wait_recv()
    total = xy_buf[0]
    for q in range(1, 16):
        total = total + xy_buf[q]
    z_own[...] = total
    z_buf[z] = total

    passes = []
    for dz in range(1, 8):
        passes.append(remote(z_own, z_buf.at[z], zsend.at[dz - 1], zrecv.at[dz - 1], z_peer(dz)))
        passes[-1].start()
    for move in passes:
        move.wait_recv()
    total = z_buf[0]
    for q in range(1, 8):
        total = total + z_buf[q]

    def slot(q):
        return pl.ds(pl.multiple_of(c * half + q * size, size), size)

    done[slot(me), :] = total
    gathers, onward = [], []
    for n, (dx, dy) in enumerate(XY_OFFSETS):
        gathers.append(remote(done.at[slot(me)], done.at[slot(me)], gsend.at[n], grecv.at[n], xy_peer(dx, dy)[1]))
        gathers[-1].start()
    for n, (dx, dy) in enumerate([(0, 0)] + XY_OFFSETS):
        if n:
            gathers[n - 1].wait_recv()
        q = lax.rem(x - dx + 4, 4) * 4 + lax.rem(y - dy + 4, 4)
        onward.append(remote(done.at[slot(q)], done.at[slot(q)], fsend.at[n], frecv.at[n], core_peer()))
        onward[-1].start()
    for move in onward:
        move.wait_recv()
    gram[...] = done[...]
    for move in moves + [swap] + outs + passes + gathers + onward:
        move.wait_send()
    for h in range(2):
        pltpu.make_async_copy(cells.at[h], cells_out.at[h], out_sem.at[h]).wait()


def triangular_inverse(small, strips):
    lane = lax.broadcasted_iota(jnp.int32, (8, 128), 1)
    sub = lax.broadcasted_iota(jnp.int32, (8, 128), 0)
    left = [small[8 * s : 8 * s + 8, :] for s in range(16)]
    right = [(lane == sub + 8 * s).astype(F32) for s in range(16)]

    def over_rows(strip, i):
        return jnp.broadcast_to(strip[i : i + 1, :], (8, 128))

    def over_lanes(strip, j):
        return jnp.broadcast_to(strip[:, j : j + 1], (8, 128))

    for k in range(16):
        rows_l = [over_rows(left[k], i) for i in range(8)]
        rows_r = [over_rows(right[k], i) for i in range(8)]
        e = [[over_lanes(rows_l[i], 8 * k + j) for j in range(i + 1)] for i in range(8)]
        columns = {s: [over_lanes(left[s], 8 * k + j) for j in range(8)] for s in range(k + 1, 16)}
        inv = []
        low = [[None] * 8 for _ in range(8)]
        for j in range(8):
            inv.append(lax.rsqrt(e[j][j]))
            for i in range(j + 1, 8):
                low[i][j] = e[i][j] * inv[j]
            for i in range(j + 1, 8):
                for m in range(j + 1, i + 1):
                    e[i][m] = e[i][m] - low[i][j] * low[m][j]

        def forward(rhs):
            out = []
            for j in range(8):
                t = rhs[j]
                for m in range(j):
                    t = t - low[j][m] * out[m]
                out.append(t * inv[j])
            return out

        u, v = forward(rows_l), forward(rows_r)
        strip = v[0]
        for j in range(1, 8):
            strip = jnp.where(sub == j, v[j], strip)
        strips[pl.ds(8 * k, 8), :] = strip
        for s in range(k + 1, 16):
            col = forward(columns[s])
            for m in range(8):
                left[s] = left[s] - col[m] * u[m]
                right[s] = right[s] - col[m] * v[m]


def factor_kernel(packed, start, basis, factor, gram, inverse):
    for n, (i, j) in enumerate(BLOCKS):
        block = packed[pl.ds(n * 128, 128), :]
        gram[pl.ds(i * 128, 128), pl.ds(j * 128, 128)] = block
        if i != j:
            gram[pl.ds(j * 128, 128), pl.ds(i * 128, 128)] = block.T
    basis[...] = start[...]

    def iterate(step, carry):
        image = dot(gram[...], basis[...], (1, 0), HIGHEST)
        small = dot(image, image, (0, 0), HIGHEST)
        triangular_inverse(small, inverse)
        basis[...] = dot(image, inverse[...], (1, 1), HIGHEST)
        return carry

    lax.fori_loop(0, ITERS, iterate, 0)
    factor[...] = basis[...] * math.sqrt(512)


def core_kernel(cells_in, basis, core, cells, stage, in_sem, own_sem, send_sem, recv_sem):
    gx, gy = lax.axis_index("gx"), lax.axis_index("gy")
    barrier = pltpu.get_barrier_semaphore()
    for dz, dy in GX_OFFSETS:
        pl.semaphore_signal(barrier, inc=1, device_id=(gx_peer(dz, dy), gy), device_id_type=MESH)
    loads = [pltpu.make_async_copy(cells_in.at[h], cells.at[h], in_sem.at[h]) for h in range(2)]
    for load in loads:
        load.start()
    flat = cells.reshape(2 * 512 * 8, 128)
    staged = stage.reshape(2 * 128 * 8, 128)
    weights = split(basis[...].T)
    moves = []
    for h in range(2):
        loads[h].wait()
        for b in range(8):
            rows = split(flat[pl.ds(h * 4096 + b, 512, stride=8), :])
            staged[pl.ds(h * 1024 + b, 128, stride=8), :] = dot3(weights, rows, (1, 0))
        if h == 0:
            pl.semaphore_wait(barrier, 15)
        cells_at = pl.ds(pl.multiple_of(gx % 2 * 16 + h * 8, 8), 8)
        for n, (dz, dy) in enumerate(GX_OFFSETS):
            home = gx_peer(dz, dy)
            ranks = pl.ds(pl.multiple_of(home * 8, 8), 8)
            moves.append(remote(stage.at[h, ranks], core.at[:, gx // 2, cells_at, :], send_sem.at[h * 15 + n], recv_sem.at[h * 15 + n], (home, gy)))
            moves[-1].start()
        own = pl.ds(pl.multiple_of(gx * 8, 8), 8)
        pltpu.make_async_copy(stage.at[h, own], core.at[:, gx // 2, cells_at, :], own_sem.at[h]).start()
    for move in moves:
        move.wait()
    for h in range(2):
        cells_at = pl.ds(pl.multiple_of(gx % 2 * 16 + h * 8, 8), 8)
        own = pl.ds(pl.multiple_of(gx * 8, 8), 8)
        pltpu.make_async_copy(stage.at[h, own], core.at[:, gx // 2, cells_at, :], own_sem.at[h]).wait()


VMEM = pl.BlockSpec(memory_space=pltpu.VMEM)
ANY = pl.BlockSpec(memory_space=pl.ANY)
DMA = pltpu.SemaphoreType.DMA
LIMIT = 48 * 2**20


def gram_call(snapshot):
    size = SLICE * 8
    return pl.pallas_call(
        gram_kernel,
        out_shape=(jax.ShapeDtypeStruct((1280, 128), F32), jax.ShapeDtypeStruct((2, 512, 8, 128), F32)),
        in_specs=[ANY],
        out_specs=(VMEM, ANY),
        scratch_shapes=[
            pltpu.VMEM((2, 512, 8, 128), F32),
            pltpu.VMEM((512, 1024), BF16),
            pltpu.VMEM((512, 1024), BF16),
            pltpu.VMEM((1280, 128), F32),
            pltpu.VMEM((640, 128), F32),
            pltpu.VMEM((640, 128), F32),
            pltpu.VMEM((16, size, 128), F32),
            pltpu.VMEM((size, 128), F32),
            pltpu.VMEM((8, size, 128), F32),
            pltpu.VMEM((1280, 128), F32),
            DMA((2,)), DMA((2,)), DMA((30,)), DMA((30,)), DMA((1,)), DMA((1,)), DMA((15,)), DMA((15,)),
            DMA((7,)), DMA((7,)), DMA((15,)), DMA((15,)), DMA((16,)), DMA((16,)),
        ],
        compiler_params=pltpu.CompilerParams(collective_id=0, has_side_effects=True, vmem_limit_bytes=LIMIT),
        name="gather_and_gram",
    )(snapshot)


def factor_call(packed, start):
    shape = jax.ShapeDtypeStruct((512, 128), F32)
    return pl.pallas_call(
        factor_kernel,
        out_shape=(shape, shape),
        in_specs=[VMEM, VMEM],
        out_specs=(VMEM, VMEM),
        scratch_shapes=[pltpu.VMEM((512, 512), F32), pltpu.VMEM((128, 128), F32)],
        compiler_params=pltpu.CompilerParams(vmem_limit_bytes=LIMIT),
        name="factorize",
    )(packed, start)


def core_call(cells, basis):
    return pl.pallas_call(
        core_kernel,
        out_shape=jax.ShapeDtypeStruct((8, 8, 32, 128), F32),
        in_specs=[ANY, VMEM],
        out_specs=ANY,
        scratch_shapes=[
            pltpu.VMEM((2, 512, 8, 128), F32),
            pltpu.VMEM((2, 128, 8, 128), F32),
            DMA((2,)), DMA((2,)), DMA((30,)), DMA((30,)),
        ],
        compiler_params=pltpu.CompilerParams(collective_id=1, has_side_effects=True, vmem_limit_bytes=LIMIT),
        name="core_and_scatter",
    )(cells, basis)


def on_device(snapshot, start_factor):
    packed, cells = gram_call(snapshot)
    basis, factor = factor_call(packed, start_factor)
    return factor, core_call(cells, basis)


def solution(mesh):
    return jax.shard_map(
        on_device,
        mesh=mesh,
        in_specs=(P(None, "gx", "gy", None), P()),
        out_specs=(P(), P("gx", None, "gy", None)),
        check_vma=False,
    )
```

```python
import functools
import math

import jax
import jax.numpy as jnp
from jax import lax
from jax.experimental import pallas as pl
from jax.experimental.pallas import tpu as pltpu
from jax.sharding import PartitionSpec as P

ITERS = 2
MESH = pl.DeviceIdType.MESH
HIGHEST = lax.Precision.HIGHEST
F32, BF16 = jnp.float32, jnp.bfloat16

GX_OFFSETS = [(dz, dy) for dz in (2, 1, 3, 0) for dy in (2, 1, 3, 0) if dz or dy]
XY_OFFSETS = [(dx, dy) for dx in (2, 1, 3, 0) for dy in (2, 1, 3, 0) if dx or dy]
Z_OFFSETS = (4, 3, 5, 2, 6, 1, 7)
BLOCKS = [(i, j) for i in range(4) for j in range(i + 1)]
SLICE = 5
STOP = 9


def dot(a, b, contract, precision=None):
    return lax.dot_general(a, b, ((contract[:1], contract[1:]), ((), ())), precision=precision, preferred_element_type=F32)


def split(x):
    hi = x.astype(BF16)
    return hi, (x - hi.astype(F32)).astype(BF16)


def dot3(a, b, contract):
    return dot(a[0], b[0], contract) + (dot(a[0], b[1], contract) + dot(a[1], b[0], contract))


def place():
    gx, gy = lax.axis_index("gx"), lax.axis_index("gy")
    return gx // 4, gx % 4, gy // 8, (gy // 2) % 4, gy % 2


def gx_peer(dz, dy):
    zh, y, _, _, _ = place()
    return lax.rem(zh + dz, 4) * 4 + lax.rem(y + dy, 4)


def xy_peer(dx, dy):
    zh, y, zl, x, c = place()
    x, y = lax.rem(x + dx, 4), lax.rem(y + dy, 4)
    return x * 4 + y, (zh * 4 + y, zl * 8 + x * 2 + c)


def z_peer(dz):
    zh, y, zl, x, c = place()
    z = lax.rem(zh * 2 + zl + dz, 8)
    return (z // 2 * 4 + y, z % 2 * 8 + x * 2 + c)


def core_peer():
    zh, y, zl, x, c = place()
    return (zh * 4 + y, zl * 8 + x * 2 + 1 - c)


def remote(src, dst, send, recv, device):
    return pltpu.make_async_remote_copy(src_ref=src, dst_ref=dst, send_sem=send, recv_sem=recv, device_id=device, device_id_type=MESH)


def rows_of(index, size):
    return pl.ds(pl.multiple_of(index * size, size), size)


def triangular_inverse(small, strips):
    lane = lax.broadcasted_iota(jnp.int32, (8, 128), 1)
    sub = lax.broadcasted_iota(jnp.int32, (8, 128), 0)
    left = [small[8 * s : 8 * s + 8, :] for s in range(16)]
    right = [(lane == sub + 8 * s).astype(F32) for s in range(16)]

    def over_rows(strip, i):
        return jnp.broadcast_to(strip[i : i + 1, :], (8, 128))

    def over_lanes(strip, j):
        return jnp.broadcast_to(strip[:, j : j + 1], (8, 128))

    for k in range(16):
        rows_l = [over_rows(left[k], i) for i in range(8)]
        rows_r = [over_rows(right[k], i) for i in range(8)]
        e = [[over_lanes(rows_l[i], 8 * k + j) for j in range(i + 1)] for i in range(8)]
        columns = {s: [over_lanes(left[s], 8 * k + j) for j in range(8)] for s in range(k + 1, 16)}
        inv = []
        low = [[None] * 8 for _ in range(8)]
        for j in range(8):
            inv.append(lax.rsqrt(e[j][j]))
            for i in range(j + 1, 8):
                low[i][j] = e[i][j] * inv[j]
            for i in range(j + 1, 8):
                for m in range(j + 1, i + 1):
                    e[i][m] = e[i][m] - low[i][j] * low[m][j]

        def forward(rhs):
            out = []
            for j in range(8):
                t = rhs[j]
                for m in range(j):
                    t = t - low[j][m] * out[m]
                out.append(t * inv[j])
            return out

        u, v = forward(rows_l), forward(rows_r)
        strip = v[0]
        for j in range(1, 8):
            strip = jnp.where(sub == j, v[j], strip)
        strips[pl.ds(8 * k, 8), :] = strip
        for s in range(k + 1, 16):
            col = forward(columns[s])
            for m in range(8):
                left[s] = left[s] - col[m] * u[m]
                right[s] = right[s] - col[m] * v[m]


def kernel(
    snap, start, factor, core,
    cells, high, low, partial, core_buf, part, xy_buf, z_own, z_buf, done, gram, basis, inverse, stage,
    local_sem, send_sem, recv_sem, csend, crecv, xsend, xrecv, zsend, zrecv, gsend, grecv, fsend, frecv,
    bsend, brecv, known,
):
    gx, gy = lax.axis_index("gx"), lax.axis_index("gy")
    zh, y, zl, x, c = place()
    z = zh * 2 + zl

    def source(home, h):
        return snap.at[home // 2, :, pl.ds(pl.multiple_of(home % 2 * 16 + h * 8, 8), 8), :]

    own = [pltpu.make_async_copy(source(gx, h), cells.at[h, rows_of(gx, 32)], local_sem.at[h]) for h in range(2)]
    near = [z_peer(2), z_peer(6), xy_peer(0, 1)[1], xy_peer(0, 3)[1], xy_peer(1, 0)[1], xy_peer(3, 0)[1]]
    barrier = pltpu.get_barrier_semaphore()
    for device in near + [z_peer(1), z_peer(7), core_peer()]:
        pl.semaphore_signal(barrier, inc=1, device_id=device, device_id_type=MESH)
    for copy in own:
        copy.start()
    pl.semaphore_wait(barrier, 9)
    moves = {}

    def send(h, n):
        dz, dy = GX_OFFSETS[n]
        home = gx_peer(dz, dy)
        moves[h, n] = remote(source(home, h), cells.at[h, rows_of(gx, 32)], send_sem.at[h * 15 + n], recv_sem.at[h * 15 + n], (home, gy))
        moves[h, n].start()

    for steps in range(1, 5):
        if steps < 4:
            for device in near:
                pl.semaphore_signal(known.at[steps - 1], inc=1, device_id=device, device_id_type=MESH)
        for n, (dz, dy) in enumerate(GX_OFFSETS):
            if min(dz, 4 - dz) + min(dy, 4 - dy) == steps:
                send(0, n)
        if steps < 4:
            pl.semaphore_wait(known.at[steps - 1], 6)
    for n in range(15):
        send(1, n)
    sent = list(moves.values())

    flat = cells.reshape(2 * 512 * 8, 128)

    def convert(h, row):
        for b in range(8):
            rows = flat[pl.ds((h * 512 + row * 32) * 8 + b, 32, stride=8), :]
            hi, lo = split(rows)
            high[h, rows_of(row, 32), pl.ds(b * 128, 128)] = hi
            low[h, rows_of(row, 32), pl.ds(b * 128, 128)] = lo

    for h in range(2):
        own[h].wait()
        if STOP >= 2:
            convert(h, gx)
        if STOP >= 1:
            for n, (dz, dy) in enumerate(GX_OFFSETS):
                moves[h, n].wait_recv()
                if STOP >= 2:
                    convert(h, gx_peer((4 - dz) % 4, (4 - dy) % 4))
        if STOP >= 3:
            for first, at in ((0, 0), (2, 256)):
                rows, cols = pl.ds(at, 512 - at), pl.ds(at, 256)
                term = dot3((high[h, rows, :], low[h, rows, :]), (high[h, cols, :], low[h, cols, :]), (1, 1))
                for n, (i, j) in enumerate(BLOCKS):
                    if j in (first, first + 1):
                        block = term[i * 128 - at : i * 128 - at + 128, (j - first) * 128 : (j - first) * 128 + 128]
                        if h:
                            block = block + partial[pl.ds(n * 128, 128), :]
                        partial[pl.ds(n * 128, 128), :] = block

    half = 80 * 8
    if STOP >= 4:
        swap = remote(partial.at[rows_of(1 - c, half)], core_buf, csend.at[0], crecv.at[0], core_peer())
        swap.start()
        sent.append(swap)
        swap.wait_recv()
        part[...] = partial[rows_of(c, half), :] + core_buf[...]

    size = SLICE * 8
    me = x * 4 + y
    if STOP >= 5:
        outs = []
        for n, (dx, dy) in enumerate(XY_OFFSETS):
            q, device = xy_peer(dx, dy)
            outs.append(remote(part.at[rows_of(q, size)], xy_buf.at[me], xsend.at[n], xrecv.at[n], device))
            outs[-1].start()
        xy_buf[me] = part[rows_of(me, size), :]
        for move in outs:
            move.wait_recv()
        sent += outs
        total = xy_buf[0]
        for q in range(1, 16):
            total = total + xy_buf[q]
        z_own[...] = total
        z_buf[z] = total

    if STOP >= 6:
        passes = []
        for n, dz in enumerate(Z_OFFSETS):
            passes.append(remote(z_own, z_buf.at[z], zsend.at[n], zrecv.at[n], z_peer(dz)))
            passes[-1].start()
        for move in passes:
            move.wait_recv()
        sent += passes
        total = z_buf[0]
        for q in range(1, 8):
            total = total + z_buf[q]

    def slot(q):
        return pl.ds(pl.multiple_of(c * half + q * size, size), size)

    if STOP >= 7:
        done[slot(me), :] = total
        gathers, onward = [], []
        for n, (dx, dy) in enumerate(XY_OFFSETS):
            gathers.append(remote(done.at[slot(me)], done.at[slot(me)], gsend.at[n], grecv.at[n], xy_peer(dx, dy)[1]))
            gathers[-1].start()
        near = [(0, 0)] + [XY_OFFSETS[n] for n in range(14, -1, -1)]
        for n, (dx, dy) in enumerate(near):
            if n:
                gathers[15 - n].wait_recv()
            q = lax.rem(x - dx + 4, 4) * 4 + lax.rem(y - dy + 4, 4)
            onward.append(remote(done.at[slot(q)], done.at[slot(q)], fsend.at[n], frecv.at[n], core_peer()))
            onward[-1].start()
        for move in onward:
            move.wait_recv()
        sent += gathers + onward

    if STOP >= 8:
        for n, (i, j) in enumerate(BLOCKS):
            block = done[pl.ds(n * 128, 128), :]
            gram[pl.ds(i * 128, 128), pl.ds(j * 128, 128)] = block
            if i != j:
                gram[pl.ds(j * 128, 128), pl.ds(i * 128, 128)] = block.T
        basis[...] = start[...]

        def iterate(step, carry):
            image = dot(gram[...], basis[...], (1, 0), HIGHEST)
            small = dot(image, image, (0, 0), HIGHEST)
            triangular_inverse(small, inverse)
            basis[...] = dot(image, inverse[...], (1, 1), HIGHEST)
            return carry

        lax.fori_loop(0, ITERS, iterate, 0)
    factor[...] = basis[...] * math.sqrt(512)

    if STOP >= 9:
        staged = stage.reshape(2 * 128 * 8, 128)
        weights = split(basis[...].T)
        backs = []
        for h in range(2):
            block = dot3(weights, (high[h], low[h]), (1, 0))
            for b in range(8):
                staged[pl.ds(h * 1024 + b, 128, stride=8), :] = block[:, b * 128 : b * 128 + 128]
            at = pl.ds(pl.multiple_of(gx % 2 * 16 + h * 8, 8), 8)
            for n, (dz, dy) in enumerate(GX_OFFSETS):
                home = gx_peer(dz, dy)
                backs.append(remote(stage.at[h, rows_of(home, 8)], core.at[:, gx // 2, at, :], bsend.at[h * 15 + n], brecv.at[h * 15 + n], (home, gy)))
                backs[-1].start()
            core[:, gx // 2, at, :] = stage[h, rows_of(gx, 8)]
        for move in backs:
            move.wait_recv()
        sent += backs
    for move in sent:
        move.wait_send()


VMEM = pl.BlockSpec(memory_space=pltpu.VMEM)
ANY = pl.BlockSpec(memory_space=pl.ANY)
DMA = pltpu.SemaphoreType.DMA


def on_device(snapshot, start_factor):
    size = SLICE * 8
    return pl.pallas_call(
        kernel,
        out_shape=(jax.ShapeDtypeStruct((512, 128), F32), jax.ShapeDtypeStruct((8, 8, 32, 128), F32)),
        in_specs=[ANY, VMEM],
        out_specs=(VMEM, VMEM),
        scratch_shapes=[
            pltpu.VMEM((2, 512, 8, 128), F32),
            pltpu.VMEM((2, 512, 1024), BF16),
            pltpu.VMEM((2, 512, 1024), BF16),
            pltpu.VMEM((1280, 128), F32),
            pltpu.VMEM((640, 128), F32),
            pltpu.VMEM((640, 128), F32),
            pltpu.VMEM((16, size, 128), F32),
            pltpu.VMEM((size, 128), F32),
            pltpu.VMEM((8, size, 128), F32),
            pltpu.VMEM((1280, 128), F32),
            pltpu.VMEM((512, 512), F32),
            pltpu.VMEM((512, 128), F32),
            pltpu.VMEM((128, 128), F32),
            pltpu.VMEM((2, 128, 8, 128), F32),
            DMA((2,)), DMA((30,)), DMA((30,)), DMA((1,)), DMA((1,)), DMA((15,)), DMA((15,)),
            DMA((7,)), DMA((7,)), DMA((15,)), DMA((15,)), DMA((16,)), DMA((16,)),
            DMA((30,)), DMA((30,)), pltpu.SemaphoreType.REGULAR((3,)),
        ],
        compiler_params=pltpu.CompilerParams(collective_id=0, has_side_effects=True, vmem_limit_bytes=48 * 2**20),
        name="hosvd_mode",
    )(snapshot, start_factor)


def solution(mesh):
    return jax.shard_map(
        on_device,
        mesh=mesh,
        in_specs=(P(None, "gx", "gy", None), P()),
        out_specs=(P(), P("gx", None, "gy", None)),
        check_vma=False,
    )
```

```python
import functools
import math

import jax
import jax.numpy as jnp
from jax import lax
from jax.experimental import pallas as pl
from jax.experimental.pallas import tpu as pltpu
from jax.sharding import PartitionSpec as P

ITERS = 2
MESH = pl.DeviceIdType.MESH
HIGHEST = lax.Precision.HIGHEST
F32, BF16 = jnp.float32, jnp.bfloat16

GX_OFFSETS = [(dz, dy) for dz in (2, 1, 3, 0) for dy in (2, 1, 3, 0) if dz or dy]
XY_OFFSETS = [(dx, dy) for dx in (2, 1, 3, 0) for dy in (2, 1, 3, 0) if dx or dy]
Z_OFFSETS = (4, 3, 5, 2, 6, 1, 7)
BLOCKS = [(i, j) for i in range(4) for j in range(i + 1)]
SLICE = 5
STOP = 9
LIMIT = 50 * 2**20


def dot(a, b, contract, precision=None):
    return lax.dot_general(a, b, ((contract[:1], contract[1:]), ((), ())), precision=precision, preferred_element_type=F32)


def split(x):
    hi = x.astype(BF16)
    return hi, (x - hi.astype(F32)).astype(BF16)


def dot3(a, b, contract):
    return dot(a[0], b[0], contract) + (dot(a[0], b[1], contract) + dot(a[1], b[0], contract))


def place():
    gx, gy = lax.axis_index("gx"), lax.axis_index("gy")
    return gx // 4, gx % 4, gy // 8, (gy // 2) % 4, gy % 2


def gx_peer(dz, dy):
    zh, y, _, _, _ = place()
    return lax.rem(zh + dz, 4) * 4 + lax.rem(y + dy, 4)


def xy_peer(dx, dy):
    zh, y, zl, x, c = place()
    x, y = lax.rem(x + dx, 4), lax.rem(y + dy, 4)
    return x * 4 + y, (zh * 4 + y, zl * 8 + x * 2 + c)


def z_peer(dz):
    zh, y, zl, x, c = place()
    z = lax.rem(zh * 2 + zl + dz, 8)
    return (z // 2 * 4 + y, z % 2 * 8 + x * 2 + c)


def core_peer():
    zh, y, zl, x, c = place()
    return (zh * 4 + y, zl * 8 + x * 2 + 1 - c)


def remote(src, dst, send, recv, device):
    return pltpu.make_async_remote_copy(src_ref=src, dst_ref=dst, send_sem=send, recv_sem=recv, device_id=device, device_id_type=MESH)


def rows_of(index, size):
    return pl.ds(pl.multiple_of(index * size, size), size)


def triangular_inverse(small, strips, after=None):
    lane = lax.broadcasted_iota(jnp.int32, (8, 128), 1)
    sub = lax.broadcasted_iota(jnp.int32, (8, 128), 0)
    work = [small[8 * s : 8 * s + 8, :] for s in range(16)]

    def over_rows(strip, i):
        return jnp.broadcast_to(strip[i : i + 1, :], (8, 128))

    def over_lanes(strip, j):
        return jnp.broadcast_to(strip[:, j : j + 1], (8, 128))

    for k in range(16):
        rows = [over_rows(work[k], i) for i in range(8)]
        e = [[over_lanes(rows[i], 8 * k + j) for j in range(i + 1)] for i in range(8)]
        columns = {s: [over_lanes(work[s], 8 * k + j) for j in range(8)] for s in range(k + 1, 16)}
        inside = (lane >= 8 * k) & (lane < 8 * k + 8)
        inv = []
        low = [[None] * 8 for _ in range(8)]
        for j in range(8):
            inv.append(lax.rsqrt(e[j][j]))
            for i in range(j + 1, 8):
                low[i][j] = e[i][j] * inv[j]
            for i in range(j + 1, 8):
                for m in range(j + 1, i + 1):
                    e[i][m] = e[i][m] - low[i][j] * low[m][j]

        def forward(rhs):
            out = []
            for j in range(8):
                t = rhs[j]
                for m in range(j):
                    t = t - low[j][m] * out[m]
                out.append(t * inv[j])
            return out

        u = forward([jnp.where(inside, (lane == 8 * k + i).astype(F32), rows[i]) for i in range(8)])
        strip = u[0]
        for j in range(1, 8):
            strip = jnp.where(sub == j, u[j], strip)
        strips[pl.ds(8 * k, 8), :] = jnp.where(lane < 8 * k + 8, strip, 0.0)
        for s in range(k + 1, 16):
            col = forward(columns[s])
            t = jnp.where(inside, 0.0, work[s])
            for m in range(8):
                t = t - col[m] * u[m]
            work[s] = t
        if after and k % 4 == 3:
            after(k // 4)


def kernel(
    snap, start, factor, core,
    cells, high, low, partial, core_buf, part, xy_buf, z_own, z_buf, done, gram, basis, turned, image, inverse, stage,
    local_sem, send_sem, recv_sem, csend, crecv, xsend, xrecv, zsend, zrecv, gsend, grecv, fsend, frecv,
    bsend, brecv, known, start_sem,
):
    gx, gy = lax.axis_index("gx"), lax.axis_index("gy")
    zh, y, zl, x, c = place()
    z = zh * 2 + zl

    def source(home, h):
        return snap.at[home // 2, :, pl.ds(pl.multiple_of(home % 2 * 16 + h * 8, 8), 8), :]

    own = [pltpu.make_async_copy(source(gx, h), cells.at[h, rows_of(gx, 32)], local_sem.at[h]) for h in range(2)]
    near = [z_peer(2), z_peer(6), xy_peer(0, 1)[1], xy_peer(0, 3)[1], xy_peer(1, 0)[1], xy_peer(3, 0)[1]]
    barrier = pltpu.get_barrier_semaphore()
    for device in near + [z_peer(1), z_peer(7), core_peer()]:
        pl.semaphore_signal(barrier, inc=1, device_id=device, device_id_type=MESH)
    begin = pltpu.make_async_copy(start, basis, start_sem.at[0])
    for copy in own + [begin]:
        copy.start()
    pl.semaphore_wait(barrier, 9)
    moves = {}

    def send(h, n):
        dz, dy = GX_OFFSETS[n]
        home = gx_peer(dz, dy)
        moves[h, n] = remote(source(home, h), cells.at[h, rows_of(gx, 32)], send_sem.at[h * 15 + n], recv_sem.at[h * 15 + n], (home, gy))
        moves[h, n].start()

    for steps in range(1, 5):
        if steps < 4:
            for device in near:
                pl.semaphore_signal(known.at[steps - 1], inc=1, device_id=device, device_id_type=MESH)
        for n, (dz, dy) in enumerate(GX_OFFSETS):
            if min(dz, 4 - dz) + min(dy, 4 - dy) == steps:
                send(0, n)
        if steps < 4:
            pl.semaphore_wait(known.at[steps - 1], 6)
    for n in range(15):
        send(1, n)
    sent = list(moves.values())

    begin.wait()
    turned[...] = basis[...].T
    flat = cells.reshape(2 * 512 * 8, 128)

    def convert(h, row):
        for b in range(8):
            rows = flat[pl.ds((h * 512 + row * 32) * 8 + b, 32, stride=8), :]
            hi, lo = split(rows)
            high[h, rows_of(row, 32), pl.ds(b * 128, 128)] = hi
            low[h, rows_of(row, 32), pl.ds(b * 128, 128)] = lo

    for h in range(2):
        own[h].wait()
        if STOP >= 2:
            convert(h, gx)
        if STOP >= 1:
            for n, (dz, dy) in enumerate(GX_OFFSETS):
                moves[h, n].wait_recv()
                if STOP >= 2:
                    convert(h, gx_peer((4 - dz) % 4, (4 - dy) % 4))
        if STOP >= 3:
            for first, at in ((0, 0), (2, 256)):
                rows, cols = pl.ds(at, 512 - at), pl.ds(at, 256)
                term = dot3((high[h, rows, :], low[h, rows, :]), (high[h, cols, :], low[h, cols, :]), (1, 1))
                for n, (i, j) in enumerate(BLOCKS):
                    if j in (first, first + 1):
                        block = term[i * 128 - at : i * 128 - at + 128, (j - first) * 128 : (j - first) * 128 + 128]
                        if h:
                            block = block + partial[pl.ds(n * 128, 128), :]
                        partial[pl.ds(n * 128, 128), :] = block

    half = 80 * 8
    if STOP >= 4:
        swap = remote(partial.at[rows_of(1 - c, half)], core_buf, csend.at[0], crecv.at[0], core_peer())
        swap.start()
        sent.append(swap)
        swap.wait_recv()
        part[...] = partial[rows_of(c, half), :] + core_buf[...]

    size = SLICE * 8
    me = x * 4 + y
    if STOP >= 5:
        outs = []
        for n, (dx, dy) in enumerate(XY_OFFSETS):
            q, device = xy_peer(dx, dy)
            outs.append(remote(part.at[rows_of(q, size)], xy_buf.at[me], xsend.at[n], xrecv.at[n], device))
            outs[-1].start()
        xy_buf[me] = part[rows_of(me, size), :]
        for move in outs:
            move.wait_recv()
        sent += outs
        total = xy_buf[0]
        for q in range(1, 16):
            total = total + xy_buf[q]
        z_own[...] = total
        z_buf[z] = total

    if STOP >= 6:
        passes = []
        for n, dz in enumerate(Z_OFFSETS):
            passes.append(remote(z_own, z_buf.at[z], zsend.at[n], zrecv.at[n], z_peer(dz)))
            passes[-1].start()
        for move in passes:
            move.wait_recv()
        sent += passes
        total = z_buf[0]
        for q in range(1, 8):
            total = total + z_buf[q]

    def slot(q):
        return pl.ds(pl.multiple_of(c * half + q * size, size), size)

    if STOP >= 7:
        done[slot(me), :] = total
        gathers, onward = [], []
        for n, (dx, dy) in enumerate(XY_OFFSETS):
            gathers.append(remote(done.at[slot(me)], done.at[slot(me)], gsend.at[n], grecv.at[n], xy_peer(dx, dy)[1]))
            gathers[-1].start()
        near = [(0, 0)] + [XY_OFFSETS[n] for n in range(14, -1, -1)]
        for n, (dx, dy) in enumerate(near):
            if n:
                gathers[15 - n].wait_recv()
            q = lax.rem(x - dx + 4, 4) * 4 + lax.rem(y - dy + 4, 4)
            onward.append(remote(done.at[slot(q)], done.at[slot(q)], fsend.at[n], frecv.at[n], core_peer()))
            onward[-1].start()
        for move in onward:
            move.wait_recv()
        sent += gathers + onward

    if STOP >= 8:
        for n, (i, j) in enumerate(BLOCKS):
            block = done[pl.ds(n * 128, 128), :]
            gram[pl.ds(i * 128, 128), pl.ds(j * 128, 128)] = block
            if i != j:
                gram[pl.ds(j * 128, 128), pl.ds(i * 128, 128)] = block.T
        staged = stage.reshape(2 * 128 * 8, 128)
        backs = []

        def cells_at(h):
            return pl.ds(pl.multiple_of(gx % 2 * 16 + h * 8, 8), 8)

        def back(h, home, n, m):
            backs.append(remote(stage.at[h, rows_of(home, 8)], core.at[:, gx // 2, cells_at(h), :], bsend.at[n], brecv.at[m], (home, gy)))
            backs[-1].start()

        def ranks_done(r):
            ranks = pl.ds(32 * r, 32)
            rows = dot(inverse[ranks, :], image[...], (1, 0), HIGHEST)
            turned[ranks, :] = rows
            weights = split(rows)
            for h in range(2):
                block = dot3(weights, (high[h], low[h]), (1, 0))
                for b in range(8):
                    staged[pl.ds(h * 1024 + r * 256 + b, 32, stride=8), :] = block[:, b * 128 : b * 128 + 128]
                for dy in (2, 1, 3):
                    back(h, r * 4 + lax.rem(y + dy, 4), 6 + (h * 4 + r) * 3 + dy - 1, 6 + (h * 4 + zh) * 3 + dy - 1)

        for step in range(ITERS):
            image[...] = dot(turned[...], gram[...], (1, 0), HIGHEST)
            small = dot(image[...], image[...], (1, 1), HIGHEST)
            if step < ITERS - 1:
                triangular_inverse(small, inverse)
                turned[...] = dot(inverse[...], image[...], (1, 0), HIGHEST)
            else:
                triangular_inverse(small, inverse, ranks_done)
        for h in range(2):
            for dz in (2, 1, 3):
                back(h, gx_peer(dz, 0), h * 3 + dz - 1, h * 3 + dz - 1)
        factor[...] = turned[...].T * math.sqrt(512)
        for h in range(2):
            core[:, gx // 2, cells_at(h), :] = stage[h, rows_of(gx, 8)]
        for move in backs[24:]:
            move.wait_recv()
        for h in range(2):
            for source_zh in range(4):
                for dy in range(1, 4):
                    m = 6 + (h * 4 + source_zh) * 3 + dy - 1
                    remote(stage.at[h, rows_of(gx, 8)], core.at[:, gx // 2, cells_at(h), :], bsend.at[m], brecv.at[m], (gx_peer(0, dy), gy)).wait_recv()
        sent += backs
    for move in sent:
        move.wait_send()


VMEM = pl.BlockSpec(memory_space=pltpu.VMEM)
ANY = pl.BlockSpec(memory_space=pl.ANY)
DMA = pltpu.SemaphoreType.DMA


def on_device(snapshot, start_factor):
    size = SLICE * 8
    outs = (jax.ShapeDtypeStruct((512, 128), F32), jax.ShapeDtypeStruct((8, 8, 32, 128), F32))
    return pl.pallas_call(
        kernel,
        out_shape=outs,
        in_specs=[ANY, ANY],
        out_specs=(VMEM, VMEM),
        scratch_shapes=[
            pltpu.VMEM((2, 512, 8, 128), F32),
            pltpu.VMEM((2, 512, 1024), BF16),
            pltpu.VMEM((2, 512, 1024), BF16),
            pltpu.VMEM((1280, 128), F32),
            pltpu.VMEM((640, 128), F32),
            pltpu.VMEM((640, 128), F32),
            pltpu.VMEM((16, size, 128), F32),
            pltpu.VMEM((size, 128), F32),
            pltpu.VMEM((8, size, 128), F32),
            pltpu.VMEM((1280, 128), F32),
            pltpu.VMEM((512, 512), F32),
            pltpu.VMEM((512, 128), F32),
            pltpu.VMEM((128, 512), F32),
            pltpu.VMEM((128, 512), F32),
            pltpu.VMEM((128, 128), F32),
            pltpu.VMEM((2, 128, 8, 128), F32),
            DMA((2,)), DMA((30,)), DMA((30,)), DMA((1,)), DMA((1,)), DMA((15,)), DMA((15,)),
            DMA((7,)), DMA((7,)), DMA((15,)), DMA((15,)), DMA((16,)), DMA((16,)),
            DMA((30,)), DMA((30,)), pltpu.SemaphoreType.REGULAR((3,)), DMA((1,)),
        ],
        compiler_params=pltpu.CompilerParams(collective_id=0, has_side_effects=True, vmem_limit_bytes=LIMIT),
        name="hosvd_mode",
    )(snapshot, start_factor)


def solution(mesh):
    return jax.shard_map(
        on_device,
        mesh=mesh,
        in_specs=(P(None, "gx", "gy", None), P()),
        out_specs=(P(), P("gx", None, "gy", None)),
        check_vma=False,
    )
```

```python
import functools
import math

import jax
import jax.numpy as jnp
from jax import lax
from jax.experimental import pallas as pl
from jax.experimental.pallas import tpu as pltpu
from jax.sharding import PartitionSpec as P

ITERS = 2
MESH = pl.DeviceIdType.MESH
HIGHEST = lax.Precision.HIGHEST
F32, BF16 = jnp.float32, jnp.bfloat16

GX_OFFSETS = [(dz, dy) for dz in (2, 1, 3, 0) for dy in (2, 1, 3, 0) if dz or dy]
XY_OFFSETS = [(dx, dy) for dx in (2, 1, 3, 0) for dy in (2, 1, 3, 0) if dx or dy]
Z_OFFSETS = (4, 3, 5, 2, 6, 1, 7)
BLOCKS = [(i, j) for i in range(4) for j in range(i + 1)]
PARTS = [(0, 16), (16, 24)]
SLICE = 5
STOP = 9
LIMIT = 50 * 2**20


def dot(a, b, contract, precision=None):
    return lax.dot_general(a, b, ((contract[:1], contract[1:]), ((), ())), precision=precision, preferred_element_type=F32)


def split(x):
    hi = x.astype(BF16)
    return hi, (x - hi.astype(F32)).astype(BF16)


def dot3(a, b, contract):
    return dot(a[0], b[0], contract) + (dot(a[0], b[1], contract) + dot(a[1], b[0], contract))


def place():
    gx, gy = lax.axis_index("gx"), lax.axis_index("gy")
    return gx // 4, gx % 4, gy // 8, (gy // 2) % 4, gy % 2


def gx_peer(dz, dy):
    zh, y, _, _, _ = place()
    return lax.rem(zh + dz, 4) * 4 + lax.rem(y + dy, 4)


def xy_peer(dx, dy):
    zh, y, zl, x, c = place()
    x, y = lax.rem(x + dx, 4), lax.rem(y + dy, 4)
    return x * 4 + y, (zh * 4 + y, zl * 8 + x * 2 + c)


def z_peer(dz):
    zh, y, zl, x, c = place()
    z = lax.rem(zh * 2 + zl + dz, 8)
    return (z // 2 * 4 + y, z % 2 * 8 + x * 2 + c)


def core_peer():
    zh, y, zl, x, c = place()
    return (zh * 4 + y, zl * 8 + x * 2 + 1 - c)


def remote(src, dst, send, recv, device):
    return pltpu.make_async_remote_copy(src_ref=src, dst_ref=dst, send_sem=send, recv_sem=recv, device_id=device, device_id_type=MESH)


def rows_of(index, size):
    return pl.ds(pl.multiple_of(index * size, size), size)


def triangular_inverse(small, strips, after=None):
    lane = lax.broadcasted_iota(jnp.int32, (8, 128), 1)
    sub = lax.broadcasted_iota(jnp.int32, (8, 128), 0)
    work = [small[8 * s : 8 * s + 8, :] for s in range(16)]

    def over_rows(strip, i):
        return jnp.broadcast_to(strip[i : i + 1, :], (8, 128))

    def over_lanes(strip, j):
        return jnp.broadcast_to(strip[:, j : j + 1], (8, 128))

    for k in range(16):
        rows = [over_rows(work[k], i) for i in range(8)]
        e = [[over_lanes(rows[i], 8 * k + j) for j in range(i + 1)] for i in range(8)]
        columns = {s: [over_lanes(work[s], 8 * k + j) for j in range(8)] for s in range(k + 1, 16)}
        inside = (lane >= 8 * k) & (lane < 8 * k + 8)
        inv = []
        low = [[None] * 8 for _ in range(8)]
        for j in range(8):
            inv.append(lax.rsqrt(e[j][j]))
            for i in range(j + 1, 8):
                low[i][j] = e[i][j] * inv[j]
            for i in range(j + 1, 8):
                for m in range(j + 1, i + 1):
                    e[i][m] = e[i][m] - low[i][j] * low[m][j]

        def forward(rhs):
            out = []
            for j in range(8):
                t = rhs[j]
                for m in range(j):
                    t = t - low[j][m] * out[m]
                out.append(t * inv[j])
            return out

        u = forward([jnp.where(inside, (lane == 8 * k + i).astype(F32), rows[i]) for i in range(8)])
        strip = u[0]
        for j in range(1, 8):
            strip = jnp.where(sub == j, u[j], strip)
        strips[pl.ds(8 * k, 8), :] = jnp.where(lane < 8 * k + 8, strip, 0.0)
        for s in range(k + 1, 16):
            col = forward(columns[s])
            t = jnp.where(inside, 0.0, work[s])
            for m in range(8):
                t = t - col[m] * u[m]
            work[s] = t
        if after and k % 4 == 3:
            after(k // 4)


def kernel(
    snap, start, factor, core,
    cells, high, low, partial, core_buf, part, xy_buf, z_own, z_buf, done, gram, basis, turned, image, inverse, stage,
    local_sem, send_sem, recv_sem, csend, crecv, xsend, xrecv, zsend, zrecv, gsend, grecv, fsend, frecv,
    bsend, brecv, known, start_sem,
):
    gx, gy = lax.axis_index("gx"), lax.axis_index("gy")
    zh, y, zl, x, c = place()
    z = zh * 2 + zl

    def source(home, h):
        return snap.at[home // 2, :, pl.ds(pl.multiple_of(home % 2 * 16 + h * 8, 8), 8), :]

    own = [pltpu.make_async_copy(source(gx, h), cells.at[h, rows_of(gx, 32)], local_sem.at[h]) for h in range(2)]
    near = [z_peer(2), z_peer(6), xy_peer(0, 1)[1], xy_peer(0, 3)[1], xy_peer(1, 0)[1], xy_peer(3, 0)[1]]
    barrier = pltpu.get_barrier_semaphore()
    for device in near + [z_peer(1), z_peer(7), core_peer()]:
        pl.semaphore_signal(barrier, inc=1, device_id=device, device_id_type=MESH)
    begin = pltpu.make_async_copy(start, basis, start_sem.at[0])
    for copy in own + [begin]:
        copy.start()
    pl.semaphore_wait(barrier, 9)
    moves = {}

    def send(h, n):
        dz, dy = GX_OFFSETS[n]
        home = gx_peer(dz, dy)
        moves[h, n] = remote(source(home, h), cells.at[h, rows_of(gx, 32)], send_sem.at[h * 15 + n], recv_sem.at[h * 15 + n], (home, gy))
        moves[h, n].start()

    for steps in range(1, 5):
        if steps < 4:
            for device in near:
                pl.semaphore_signal(known.at[steps - 1], inc=1, device_id=device, device_id_type=MESH)
        for n, (dz, dy) in enumerate(GX_OFFSETS):
            if min(dz, 4 - dz) + min(dy, 4 - dy) == steps:
                send(0, n)
        if steps < 4:
            pl.semaphore_wait(known.at[steps - 1], 6)
    for n in range(15):
        send(1, n)
    sent = list(moves.values())

    begin.wait()
    turned[...] = basis[...].T
    flat = cells.reshape(2 * 512 * 8, 128)

    def convert(h, row):
        for b in range(8):
            rows = flat[pl.ds((h * 512 + row * 32) * 8 + b, 32, stride=8), :]
            hi, lo = split(rows)
            high[h, rows_of(row, 32), pl.ds(b * 128, 128)] = hi
            low[h, rows_of(row, 32), pl.ds(b * 128, 128)] = lo

    for h in range(2):
        own[h].wait()
        if STOP >= 2:
            convert(h, gx)
        if STOP >= 1:
            for n, (dz, dy) in enumerate(GX_OFFSETS):
                moves[h, n].wait_recv()
                if STOP >= 2:
                    convert(h, gx_peer((4 - dz) % 4, (4 - dy) % 4))
        if STOP >= 3:
            for first, at in ((0, 0), (2, 256)):
                rows, cols = pl.ds(at, 512 - at), pl.ds(at, 256)
                term = dot3((high[h, rows, :], low[h, rows, :]), (high[h, cols, :], low[h, cols, :]), (1, 1))
                for n, (i, j) in enumerate(BLOCKS):
                    if j in (first, first + 1):
                        block = term[i * 128 - at : i * 128 - at + 128, (j - first) * 128 : (j - first) * 128 + 128]
                        if h:
                            block = block + partial[pl.ds(n * 128, 128), :]
                        partial[pl.ds(n * 128, 128), :] = block

    half = 80 * 8
    if STOP >= 4:
        swap = remote(partial.at[rows_of(1 - c, half)], core_buf, csend.at[0], crecv.at[0], core_peer())
        swap.start()
        sent.append(swap)
        swap.wait_recv()
        part[...] = partial[rows_of(c, half), :] + core_buf[...]

    size = SLICE * 8
    me = x * 4 + y
    outs, passes, gathers, onward = {}, {}, {}, {}
    for p, (at, rows) in enumerate(PARTS):
        for n, (dx, dy) in enumerate(XY_OFFSETS):
            q, device = xy_peer(dx, dy)
            piece = part.at[pl.ds(pl.multiple_of(q * size + at, 8), rows)]
            outs[p, n] = remote(piece, xy_buf.at[me, pl.ds(at, rows)], xsend.at[p * 15 + n], xrecv.at[p * 15 + n], device)
            outs[p, n].start()
    xy_buf[me] = part[rows_of(me, size), :]
    for p, (at, rows) in enumerate(PARTS):
        for n in range(15):
            outs[p, n].wait_recv()
        total = xy_buf[0, pl.ds(at, rows), :]
        for q in range(1, 16):
            total = total + xy_buf[q, pl.ds(at, rows), :]
        z_buf[z, pl.ds(at, rows), :] = total
        z_own[pl.ds(at, rows), :] = total
        for n, dz in enumerate(Z_OFFSETS):
            passes[p, n] = remote(z_own.at[pl.ds(at, rows)], z_buf.at[z, pl.ds(at, rows)], zsend.at[p * 7 + n], zrecv.at[p * 7 + n], z_peer(dz))
            passes[p, n].start()

    def slot(q, p):
        at, rows = PARTS[p]
        return done.at[pl.ds(pl.multiple_of(c * half + q * size + at, 8), rows)]

    for p, (at, rows) in enumerate(PARTS):
        for n in range(7):
            passes[p, n].wait_recv()
        total = z_buf[0, pl.ds(at, rows), :]
        for q in range(1, 8):
            total = total + z_buf[q, pl.ds(at, rows), :]
        done[pl.ds(pl.multiple_of(c * half + me * size + at, 8), rows), :] = total
        for n, (dx, dy) in enumerate(XY_OFFSETS):
            gathers[p, n] = remote(slot(me, p), slot(me, p), gsend.at[p * 15 + n], grecv.at[p * 15 + n], xy_peer(dx, dy)[1])
            gathers[p, n].start()
    near = [(0, 0)] + [XY_OFFSETS[n] for n in range(14, -1, -1)]
    for p in range(len(PARTS)):
        for n, (dx, dy) in enumerate(near):
            if n:
                gathers[p, 15 - n].wait_recv()
            q = lax.rem(x - dx + 4, 4) * 4 + lax.rem(y - dy + 4, 4)
            onward[p, n] = remote(slot(q, p), slot(q, p), fsend.at[p * 16 + n], frecv.at[p * 16 + n], core_peer())
            onward[p, n].start()
    for move in onward.values():
        move.wait_recv()
    sent += [*outs.values(), *passes.values(), *gathers.values(), *onward.values()]

    if STOP >= 8:
        for n, (i, j) in enumerate(BLOCKS):
            block = done[pl.ds(n * 128, 128), :]
            gram[pl.ds(i * 128, 128), pl.ds(j * 128, 128)] = block
            if i != j:
                gram[pl.ds(j * 128, 128), pl.ds(i * 128, 128)] = block.T
        staged = stage.reshape(2 * 128 * 8, 128)
        backs = []

        def cells_at(h):
            return pl.ds(pl.multiple_of(gx % 2 * 16 + h * 8, 8), 8)

        def back(h, home, n, m):
            backs.append(remote(stage.at[h, rows_of(home, 8)], core.at[:, gx // 2, cells_at(h), :], bsend.at[n], brecv.at[m], (home, gy)))
            backs[-1].start()

        def ranks_done(r):
            ranks = pl.ds(32 * r, 32)
            rows = dot(inverse[ranks, :], image[...], (1, 0), HIGHEST)
            turned[ranks, :] = rows
            weights = split(rows)
            for h in range(2):
                block = dot3(weights, (high[h], low[h]), (1, 0))
                for b in range(8):
                    staged[pl.ds(h * 1024 + r * 256 + b, 32, stride=8), :] = block[:, b * 128 : b * 128 + 128]
                for dy in (2, 1, 3):
                    back(h, r * 4 + lax.rem(y + dy, 4), 6 + (h * 4 + r) * 3 + dy - 1, 6 + (h * 4 + zh) * 3 + dy - 1)

        for step in range(ITERS):
            image[...] = dot(turned[...], gram[...], (1, 0), HIGHEST)
            small = dot(image[...], image[...], (1, 1), HIGHEST)
            if step < ITERS - 1:
                triangular_inverse(small, inverse)
                turned[...] = dot(inverse[...], image[...], (1, 0), HIGHEST)
            else:
                triangular_inverse(small, inverse, ranks_done)
        for h in range(2):
            for dz in (2, 1, 3):
                back(h, gx_peer(dz, 0), h * 3 + dz - 1, h * 3 + dz - 1)
        factor[...] = turned[...].T * math.sqrt(512)
        for h in range(2):
            core[:, gx // 2, cells_at(h), :] = stage[h, rows_of(gx, 8)]
        for move in backs[24:]:
            move.wait_recv()
        for h in range(2):
            for source_zh in range(4):
                for dy in range(1, 4):
                    m = 6 + (h * 4 + source_zh) * 3 + dy - 1
                    remote(stage.at[h, rows_of(gx, 8)], core.at[:, gx // 2, cells_at(h), :], bsend.at[m], brecv.at[m], (gx_peer(0, dy), gy)).wait_recv()
        sent += backs
    for move in sent:
        move.wait_send()


VMEM = pl.BlockSpec(memory_space=pltpu.VMEM)
ANY = pl.BlockSpec(memory_space=pl.ANY)
DMA = pltpu.SemaphoreType.DMA


def on_device(snapshot, start_factor):
    size = SLICE * 8
    outs = (jax.ShapeDtypeStruct((512, 128), F32), jax.ShapeDtypeStruct((8, 8, 32, 128), F32))
    return pl.pallas_call(
        kernel,
        out_shape=outs,
        in_specs=[ANY, ANY],
        out_specs=(VMEM, VMEM),
        scratch_shapes=[
            pltpu.VMEM((2, 512, 8, 128), F32),
            pltpu.VMEM((2, 512, 1024), BF16),
            pltpu.VMEM((2, 512, 1024), BF16),
            pltpu.VMEM((1280, 128), F32),
            pltpu.VMEM((640, 128), F32),
            pltpu.VMEM((640, 128), F32),
            pltpu.VMEM((16, size, 128), F32),
            pltpu.VMEM((size, 128), F32),
            pltpu.VMEM((8, size, 128), F32),
            pltpu.VMEM((1280, 128), F32),
            pltpu.VMEM((512, 512), F32),
            pltpu.VMEM((512, 128), F32),
            pltpu.VMEM((128, 512), F32),
            pltpu.VMEM((128, 512), F32),
            pltpu.VMEM((128, 128), F32),
            pltpu.VMEM((2, 128, 8, 128), F32),
            DMA((2,)), DMA((30,)), DMA((30,)), DMA((1,)), DMA((1,)), DMA((30,)), DMA((30,)),
            DMA((14,)), DMA((14,)), DMA((30,)), DMA((30,)), DMA((32,)), DMA((32,)),
            DMA((30,)), DMA((30,)), pltpu.SemaphoreType.REGULAR((3,)), DMA((1,)),
        ],
        compiler_params=pltpu.CompilerParams(collective_id=0, has_side_effects=True, vmem_limit_bytes=LIMIT),
        name="hosvd_mode",
    )(snapshot, start_factor)


def solution(mesh):
    return jax.shard_map(
        on_device,
        mesh=mesh,
        in_specs=(P(None, "gx", "gy", None), P()),
        out_specs=(P(), P("gx", None, "gy", None)),
        check_vma=False,
    )
```

```python
import functools
import math

import jax
import jax.numpy as jnp
from jax import lax
from jax.experimental import pallas as pl
from jax.experimental.pallas import tpu as pltpu
from jax.sharding import PartitionSpec as P

ITERS = 2
MESH = pl.DeviceIdType.MESH
HIGHEST = lax.Precision.HIGHEST
F32, BF16 = jnp.float32, jnp.bfloat16

GX_OFFSETS = [(dz, dy) for dz in (2, 1, 3, 0) for dy in (2, 1, 3, 0) if dz or dy]
XY_OFFSETS = [(dx, dy) for dx in (2, 1, 3, 0) for dy in (2, 1, 3, 0) if dx or dy]
Z_OFFSETS = (4, 3, 5, 2, 6, 1, 7)
BLOCKS = [(i, j) for i in range(4) for j in range(i + 1)]
PARTS = [(0, 16), (16, 24)]
SLICE = 5
STOP = 9
LIMIT = 50 * 2**20


def dot(a, b, contract, precision=None):
    return lax.dot_general(a, b, ((contract[:1], contract[1:]), ((), ())), precision=precision, preferred_element_type=F32)


def split(x):
    hi = x.astype(BF16)
    return hi, (x - hi.astype(F32)).astype(BF16)


def dot3(a, b, contract):
    return dot(a[0], b[0], contract) + (dot(a[0], b[1], contract) + dot(a[1], b[0], contract))


def place():
    gx, gy = lax.axis_index("gx"), lax.axis_index("gy")
    return gx // 4, gx % 4, gy // 8, (gy // 2) % 4, gy % 2


def gx_peer(dz, dy):
    zh, y, _, _, _ = place()
    return lax.rem(zh + dz, 4) * 4 + lax.rem(y + dy, 4)


def xy_peer(dx, dy):
    zh, y, zl, x, c = place()
    x, y = lax.rem(x + dx, 4), lax.rem(y + dy, 4)
    return x * 4 + y, (zh * 4 + y, zl * 8 + x * 2 + c)


def z_peer(dz):
    zh, y, zl, x, c = place()
    z = lax.rem(zh * 2 + zl + dz, 8)
    return (z // 2 * 4 + y, z % 2 * 8 + x * 2 + c)


def core_peer():
    zh, y, zl, x, c = place()
    return (zh * 4 + y, zl * 8 + x * 2 + 1 - c)


def remote(src, dst, send, recv, device):
    return pltpu.make_async_remote_copy(src_ref=src, dst_ref=dst, send_sem=send, recv_sem=recv, device_id=device, device_id_type=MESH)


def rows_of(index, size):
    return pl.ds(pl.multiple_of(index * size, size), size)


def triangular_inverse(small, strips, after=None):
    lane = lax.broadcasted_iota(jnp.int32, (8, 128), 1)
    sub = lax.broadcasted_iota(jnp.int32, (8, 128), 0)
    work = [small[8 * s : 8 * s + 8, :] for s in range(16)]

    def over_rows(strip, i):
        return jnp.broadcast_to(strip[i : i + 1, :], (8, 128))

    def over_lanes(strip, j):
        return jnp.broadcast_to(strip[:, j : j + 1], (8, 128))

    for k in range(16):
        rows = [over_rows(work[k], i) for i in range(8)]
        e = [[over_lanes(rows[i], 8 * k + j) for j in range(i + 1)] for i in range(8)]
        columns = {s: [over_lanes(work[s], 8 * k + j) for j in range(8)] for s in range(k + 1, 16)}
        inside = (lane >= 8 * k) & (lane < 8 * k + 8)
        inv = []
        low = [[None] * 8 for _ in range(8)]
        for j in range(8):
            inv.append(lax.rsqrt(e[j][j]))
            for i in range(j + 1, 8):
                low[i][j] = e[i][j] * inv[j]
            for i in range(j + 1, 8):
                for m in range(j + 1, i + 1):
                    e[i][m] = e[i][m] - low[i][j] * low[m][j]

        def forward(rhs):
            out = []
            for j in range(8):
                t = rhs[j]
                for m in range(j):
                    t = t - low[j][m] * out[m]
                out.append(t * inv[j])
            return out

        u = forward([jnp.where(inside, (lane == 8 * k + i).astype(F32), rows[i]) for i in range(8)])
        strip = u[0]
        for j in range(1, 8):
            strip = jnp.where(sub == j, u[j], strip)
        strips[pl.ds(8 * k, 8), :] = jnp.where(lane < 8 * k + 8, strip, 0.0)
        for s in range(k + 1, 16):
            col = forward(columns[s])
            t = jnp.where(inside, 0.0, work[s])
            for m in range(8):
                t = t - col[m] * u[m]
            work[s] = t
        if after and k % 4 == 3:
            after(k // 4)


def kernel(
    snap, start, factor, core,
    cells, high, low, partial, core_buf, part, xy_buf, z_own, z_buf, done, gram, basis, turned, image, inverse, stage,
    local_sem, send_sem, recv_sem, csend, crecv, xsend, xrecv, zsend, zrecv, gsend, grecv, fsend, frecv,
    bsend, brecv, known, start_sem,
):
    gx, gy = lax.axis_index("gx"), lax.axis_index("gy")
    zh, y, zl, x, c = place()
    z = zh * 2 + zl

    def source(home, h):
        return snap.at[home // 2, :, pl.ds(pl.multiple_of(home % 2 * 16 + h * 8, 8), 8), :]

    own = [pltpu.make_async_copy(source(gx, h), cells.at[h, rows_of(gx, 32)], local_sem.at[h]) for h in range(2)]
    near = [z_peer(2), z_peer(6), xy_peer(0, 1)[1], xy_peer(0, 3)[1], xy_peer(1, 0)[1], xy_peer(3, 0)[1]]
    barrier = pltpu.get_barrier_semaphore()
    for device in near + [z_peer(1), z_peer(7), core_peer()]:
        pl.semaphore_signal(barrier, inc=1, device_id=device, device_id_type=MESH)
    begin = pltpu.make_async_copy(start, basis, start_sem.at[0])
    for copy in own + [begin]:
        copy.start()
    pl.semaphore_wait(barrier, 9)
    moves = {}

    def send(h, n):
        dz, dy = GX_OFFSETS[n]
        home = gx_peer(dz, dy)
        moves[h, n] = remote(source(home, h), cells.at[h, rows_of(gx, 32)], send_sem.at[h * 15 + n], recv_sem.at[h * 15 + n], (home, gy))
        moves[h, n].start()

    for steps in range(1, 5):
        if steps < 4:
            for device in near:
                pl.semaphore_signal(known.at[steps - 1], inc=1, device_id=device, device_id_type=MESH)
        for n, (dz, dy) in enumerate(GX_OFFSETS):
            if min(dz, 4 - dz) + min(dy, 4 - dy) == steps:
                send(0, n)
        if steps < 4:
            pl.semaphore_wait(known.at[steps - 1], 6)
    for n in range(15):
        send(1, n)
    sent = list(moves.values())

    begin.wait()
    turned[...] = basis[...].T
    flat = cells.reshape(2 * 512 * 8, 128)

    def convert(h, row):
        for b in range(8):
            rows = flat[pl.ds((h * 512 + row * 32) * 8 + b, 32, stride=8), :]
            hi, lo = split(rows)
            high[h, rows_of(row, 32), pl.ds(b * 128, 128)] = hi
            low[h, rows_of(row, 32), pl.ds(b * 128, 128)] = lo

    for h in range(2):
        own[h].wait()
        if STOP >= 2:
            convert(h, gx)
        if STOP >= 1:
            for n, (dz, dy) in enumerate(GX_OFFSETS):
                moves[h, n].wait_recv()
                if STOP >= 2:
                    convert(h, gx_peer((4 - dz) % 4, (4 - dy) % 4))
        if STOP >= 3:
            for first, at in ((0, 0), (2, 256)):
                rows, cols = pl.ds(at, 512 - at), pl.ds(at, 256)
                term = dot3((high[h, rows, :], low[h, rows, :]), (high[h, cols, :], low[h, cols, :]), (1, 1))
                for n, (i, j) in enumerate(BLOCKS):
                    if j in (first, first + 1):
                        block = term[i * 128 - at : i * 128 - at + 128, (j - first) * 128 : (j - first) * 128 + 128]
                        if h:
                            block = block + partial[pl.ds(n * 128, 128), :]
                        partial[pl.ds(n * 128, 128), :] = block

    half = 80 * 8
    if STOP >= 4:
        swap = remote(partial.at[rows_of(1 - c, half)], core_buf, csend.at[0], crecv.at[0], core_peer())
        swap.start()
        sent.append(swap)
        swap.wait_recv()
        part[...] = partial[rows_of(c, half), :] + core_buf[...]

    size = SLICE * 8
    me = x * 4 + y
    outs, passes, gathers, onward = {}, {}, {}, {}
    for p, (at, rows) in enumerate(PARTS):
        for n, (dx, dy) in enumerate(XY_OFFSETS):
            q, device = xy_peer(dx, dy)
            piece = part.at[pl.ds(pl.multiple_of(q * size + at, 8), rows)]
            outs[p, n] = remote(piece, xy_buf.at[me, pl.ds(at, rows)], xsend.at[p * 15 + n], xrecv.at[p * 15 + n], device)
            outs[p, n].start()
    xy_buf[me] = part[rows_of(me, size), :]
    for p, (at, rows) in enumerate(PARTS):
        for n in range(15):
            outs[p, n].wait_recv()
        total = xy_buf[0, pl.ds(at, rows), :]
        for q in range(1, 16):
            total = total + xy_buf[q, pl.ds(at, rows), :]
        z_buf[z, pl.ds(at, rows), :] = total
        z_own[pl.ds(at, rows), :] = total
        for n, dz in enumerate(Z_OFFSETS):
            passes[p, n] = remote(z_own.at[pl.ds(at, rows)], z_buf.at[z, pl.ds(at, rows)], zsend.at[p * 7 + n], zrecv.at[p * 7 + n], z_peer(dz))
            passes[p, n].start()

    def slot(q, p):
        at, rows = PARTS[p]
        return done.at[pl.ds(pl.multiple_of(c * half + q * size + at, 8), rows)]

    for p, (at, rows) in enumerate(PARTS):
        for n in range(7):
            passes[p, n].wait_recv()
        total = z_buf[0, pl.ds(at, rows), :]
        for q in range(1, 8):
            total = total + z_buf[q, pl.ds(at, rows), :]
        done[pl.ds(pl.multiple_of(c * half + me * size + at, 8), rows), :] = total
        for n, (dx, dy) in enumerate(XY_OFFSETS):
            gathers[p, n] = remote(slot(me, p), slot(me, p), gsend.at[p * 15 + n], grecv.at[p * 15 + n], xy_peer(dx, dy)[1])
            gathers[p, n].start()
    near = [(0, 0)] + [XY_OFFSETS[n] for n in range(14, -1, -1)]
    for p in range(len(PARTS)):
        for n, (dx, dy) in enumerate(near):
            if n:
                gathers[p, 15 - n].wait_recv()
            q = lax.rem(x - dx + 4, 4) * 4 + lax.rem(y - dy + 4, 4)
            onward[p, n] = remote(slot(q, p), slot(q, p), fsend.at[p * 16 + n], frecv.at[p * 16 + n], core_peer())
            onward[p, n].start()
    for move in onward.values():
        move.wait_recv()
    sent += [*outs.values(), *passes.values(), *gathers.values(), *onward.values()]

    if STOP >= 8:
        for n, (i, j) in enumerate(BLOCKS):
            block = done[pl.ds(n * 128, 128), :]
            gram[pl.ds(i * 128, 128), pl.ds(j * 128, 128)] = block
            if i != j:
                gram[pl.ds(j * 128, 128), pl.ds(i * 128, 128)] = block.T
        staged = stage.reshape(2 * 128 * 8, 128)
        backs = []

        def cells_at(h):
            return pl.ds(pl.multiple_of(gx % 2 * 16 + h * 8, 8), 8)

        def back(h, home, n, m):
            backs.append(remote(stage.at[h, rows_of(home, 8)], core.at[:, gx // 2, cells_at(h), :], bsend.at[n], brecv.at[m], (home, gy)))
            backs[-1].start()

        def ranks_done(r):
            ranks = pl.ds(32 * r, 32)
            rows = dot(inverse[ranks, :], image[...], (1, 0), HIGHEST)
            turned[ranks, :] = rows
            weights = split(rows)
            for h in range(2):
                block = dot3(weights, (high[h], low[h]), (1, 0))
                for b in range(8):
                    staged[pl.ds(h * 1024 + r * 256 + b, 32, stride=8), :] = block[:, b * 128 : b * 128 + 128]
                for dy in (2, 1, 3):
                    back(h, r * 4 + lax.rem(y + dy, 4), 6 + (h * 4 + r) * 3 + dy - 1, 6 + (h * 4 + zh) * 3 + dy - 1)

        image[...] = dot(turned[...], gram[...], (1, 0), HIGHEST)
        for step in range(ITERS):
            small = dot(image[...], image[...], (1, 1), HIGHEST)
            if step < ITERS - 1:
                ahead = dot(image[...], gram[...], (1, 0), HIGHEST)
                triangular_inverse(small, inverse)
                image[...] = dot(inverse[...], ahead, (1, 0), HIGHEST)
            else:
                triangular_inverse(small, inverse, ranks_done)
        for h in range(2):
            for dz in (2, 1, 3):
                back(h, gx_peer(dz, 0), h * 3 + dz - 1, h * 3 + dz - 1)
        factor[...] = turned[...].T * math.sqrt(512)
        for h in range(2):
            core[:, gx // 2, cells_at(h), :] = stage[h, rows_of(gx, 8)]
        for move in backs[24:]:
            move.wait_recv()
        for h in range(2):
            for source_zh in range(4):
                for dy in range(1, 4):
                    m = 6 + (h * 4 + source_zh) * 3 + dy - 1
                    remote(stage.at[h, rows_of(gx, 8)], core.at[:, gx // 2, cells_at(h), :], bsend.at[m], brecv.at[m], (gx_peer(0, dy), gy)).wait_recv()
        sent += backs
    for move in sent:
        move.wait_send()


VMEM = pl.BlockSpec(memory_space=pltpu.VMEM)
ANY = pl.BlockSpec(memory_space=pl.ANY)
DMA = pltpu.SemaphoreType.DMA


def finish(factor_in, core_in, factor, core, sems):
    copies = [pltpu.make_async_copy(core_in, core, sems.at[0]), pltpu.make_async_copy(factor_in, factor, sems.at[1])]
    for copy in copies:
        copy.start()
    for copy in copies:
        copy.wait()


def on_device(snapshot, start_factor):
    size = SLICE * 8
    outs = (jax.ShapeDtypeStruct((512, 128), F32), jax.ShapeDtypeStruct((8, 8, 32, 128), F32))
    results = pl.pallas_call(
        kernel,
        out_shape=outs,
        in_specs=[ANY, ANY],
        out_specs=(VMEM, VMEM),
        scratch_shapes=[
            pltpu.VMEM((2, 512, 8, 128), F32),
            pltpu.VMEM((2, 512, 1024), BF16),
            pltpu.VMEM((2, 512, 1024), BF16),
            pltpu.VMEM((1280, 128), F32),
            pltpu.VMEM((640, 128), F32),
            pltpu.VMEM((640, 128), F32),
            pltpu.VMEM((16, size, 128), F32),
            pltpu.VMEM((size, 128), F32),
            pltpu.VMEM((8, size, 128), F32),
            pltpu.VMEM((1280, 128), F32),
            pltpu.VMEM((512, 512), F32),
            pltpu.VMEM((512, 128), F32),
            pltpu.VMEM((128, 512), F32),
            pltpu.VMEM((128, 512), F32),
            pltpu.VMEM((128, 128), F32),
            pltpu.VMEM((2, 128, 8, 128), F32),
            DMA((2,)), DMA((30,)), DMA((30,)), DMA((1,)), DMA((1,)), DMA((30,)), DMA((30,)),
            DMA((14,)), DMA((14,)), DMA((30,)), DMA((30,)), DMA((32,)), DMA((32,)),
            DMA((30,)), DMA((30,)), pltpu.SemaphoreType.REGULAR((3,)), DMA((1,)),
        ],
        compiler_params=pltpu.CompilerParams(collective_id=0, has_side_effects=True, vmem_limit_bytes=LIMIT),
        name="hosvd_mode",
    )(snapshot, start_factor)
    return pl.pallas_call(
        finish,
        out_shape=outs,
        in_specs=[ANY, ANY],
        out_specs=(ANY, ANY),
        scratch_shapes=[DMA((2,))],
        compiler_params=pltpu.CompilerParams(vmem_limit_bytes=2**20),
        name="finish",
    )(*results)


def solution(mesh):
    return jax.shard_map(
        on_device,
        mesh=mesh,
        in_specs=(P(None, "gx", "gy", None), P()),
        out_specs=(P(), P("gx", None, "gy", None)),
        check_vma=False,
    )
```

```python
import functools
import math

import jax
import jax.numpy as jnp
from jax import lax
from jax.experimental import pallas as pl
from jax.experimental.pallas import tpu as pltpu
from jax.sharding import PartitionSpec as P

ITERS = 2
MESH = pl.DeviceIdType.MESH
HIGHEST = lax.Precision.HIGHEST
F32, BF16 = jnp.float32, jnp.bfloat16

GX_OFFSETS = [(dz, dy) for dz in (2, 1, 3, 0) for dy in (2, 1, 3, 0) if dz or dy]
XY_OFFSETS = [(dx, dy) for dx in (2, 1, 3, 0) for dy in (2, 1, 3, 0) if dx or dy]
Z_OFFSETS = (4, 3, 5, 2, 6, 1, 7)
BLOCKS = [(i, j) for i in range(4) for j in range(i + 1)]
PARTS = [(0, 16), (16, 24)]
SLICE = 5
STOP = 9
LIMIT = 50 * 2**20


def dot(a, b, contract, precision=None):
    return lax.dot_general(a, b, ((contract[:1], contract[1:]), ((), ())), precision=precision, preferred_element_type=F32)


def split(x):
    hi = x.astype(BF16)
    return hi, (x - hi.astype(F32)).astype(BF16)


def dot3(a, b, contract):
    return dot(a[0], b[0], contract) + (dot(a[0], b[1], contract) + dot(a[1], b[0], contract))


def place():
    gx, gy = lax.axis_index("gx"), lax.axis_index("gy")
    return gx // 4, gx % 4, gy // 8, (gy // 2) % 4, gy % 2


def gx_peer(dz, dy):
    zh, y, _, _, _ = place()
    return lax.rem(zh + dz, 4) * 4 + lax.rem(y + dy, 4)


def xy_peer(dx, dy):
    zh, y, zl, x, c = place()
    x, y = lax.rem(x + dx, 4), lax.rem(y + dy, 4)
    return x * 4 + y, (zh * 4 + y, zl * 8 + x * 2 + c)


def z_peer(dz):
    zh, y, zl, x, c = place()
    z = lax.rem(zh * 2 + zl + dz, 8)
    return (z // 2 * 4 + y, z % 2 * 8 + x * 2 + c)


def core_peer():
    zh, y, zl, x, c = place()
    return (zh * 4 + y, zl * 8 + x * 2 + 1 - c)


def remote(src, dst, send, recv, device):
    return pltpu.make_async_remote_copy(src_ref=src, dst_ref=dst, send_sem=send, recv_sem=recv, device_id=device, device_id_type=MESH)


def rows_of(index, size):
    return pl.ds(pl.multiple_of(index * size, size), size)


def triangular_inverse(small, strips, after=None):
    lane = lax.broadcasted_iota(jnp.int32, (8, 128), 1)
    sub = lax.broadcasted_iota(jnp.int32, (8, 128), 0)
    work = [small[8 * s : 8 * s + 8, :] for s in range(16)]

    def over_rows(strip, i):
        return jnp.broadcast_to(strip[i : i + 1, :], (8, 128))

    def over_lanes(strip, j):
        return jnp.broadcast_to(strip[:, j : j + 1], (8, 128))

    for k in range(16):
        rows = [over_rows(work[k], i) for i in range(8)]
        e = [[over_lanes(rows[i], 8 * k + j) for j in range(i + 1)] for i in range(8)]
        columns = {s: [over_lanes(work[s], 8 * k + j) for j in range(8)] for s in range(k + 1, 16)}
        inside = (lane >= 8 * k) & (lane < 8 * k + 8)
        inv = []
        low = [[None] * 8 for _ in range(8)]
        for j in range(8):
            inv.append(lax.rsqrt(e[j][j]))
            for i in range(j + 1, 8):
                low[i][j] = e[i][j] * inv[j]
            for i in range(j + 1, 8):
                for m in range(j + 1, i + 1):
                    e[i][m] = e[i][m] - low[i][j] * low[m][j]

        def forward(rhs):
            out = []
            for j in range(8):
                t = rhs[j]
                for m in range(j):
                    t = t - low[j][m] * out[m]
                out.append(t * inv[j])
            return out

        u = forward([jnp.where(inside, (lane == 8 * k + i).astype(F32), rows[i]) for i in range(8)])
        strip = u[0]
        for j in range(1, 8):
            strip = jnp.where(sub == j, u[j], strip)
        strips[pl.ds(8 * k, 8), :] = jnp.where(lane < 8 * k + 8, strip, 0.0)
        for s in range(k + 1, 16):
            col = forward(columns[s])
            t = jnp.where(inside, 0.0, work[s])
            for m in range(8):
                t = t - col[m] * u[m]
            work[s] = t
        if after and k % 4 == 3:
            after(k // 4)


def kernel(
    snap, start, factor, core,
    cells, high, low, partial, core_buf, part, xy_buf, z_own, z_buf, done, gram, basis, turned, image, inverse, stage,
    local_sem, send_sem, recv_sem, csend, crecv, xsend, xrecv, zsend, zrecv, gsend, grecv, fsend, frecv,
    bsend, brecv, known, start_sem,
):
    gx, gy = lax.axis_index("gx"), lax.axis_index("gy")
    zh, y, zl, x, c = place()
    z = zh * 2 + zl

    def source(home, h):
        return snap.at[home // 2, :, pl.ds(pl.multiple_of(home % 2 * 16 + h * 8, 8), 8), :]

    own = [pltpu.make_async_copy(source(gx, h), cells.at[h, rows_of(gx, 32)], local_sem.at[h]) for h in range(2)]
    near = [z_peer(2), z_peer(6), xy_peer(0, 1)[1], xy_peer(0, 3)[1], xy_peer(1, 0)[1], xy_peer(3, 0)[1]]
    barrier = pltpu.get_barrier_semaphore()
    for device in near + [z_peer(1), z_peer(7), core_peer()]:
        pl.semaphore_signal(barrier, inc=1, device_id=device, device_id_type=MESH)
    begin = pltpu.make_async_copy(start, basis, start_sem.at[0])
    for copy in own + [begin]:
        copy.start()
    pl.semaphore_wait(barrier, 9)
    moves = {}

    def send(h, n):
        dz, dy = GX_OFFSETS[n]
        home = gx_peer(dz, dy)
        moves[h, n] = remote(source(home, h), cells.at[h, rows_of(gx, 32)], send_sem.at[h * 15 + n], recv_sem.at[h * 15 + n], (home, gy))
        moves[h, n].start()

    for steps in range(1, 5):
        if steps < 4:
            for device in near:
                pl.semaphore_signal(known.at[steps - 1], inc=1, device_id=device, device_id_type=MESH)
        for n, (dz, dy) in enumerate(GX_OFFSETS):
            if min(dz, 4 - dz) + min(dy, 4 - dy) == steps:
                send(0, n)
        if steps < 4:
            pl.semaphore_wait(known.at[steps - 1], 6)
    for n in range(15):
        send(1, n)
    sent = list(moves.values())

    begin.wait()
    turned[...] = basis[...].T
    flat = cells.reshape(2 * 512 * 8, 128)

    def convert(h, row):
        for b in range(8):
            rows = flat[pl.ds((h * 512 + row * 32) * 8 + b, 32, stride=8), :]
            hi, lo = split(rows)
            high[h, rows_of(row, 32), pl.ds(b * 128, 128)] = hi
            low[h, rows_of(row, 32), pl.ds(b * 128, 128)] = lo

    for h in range(2):
        own[h].wait()
        if STOP >= 2:
            convert(h, gx)
        if STOP >= 1:
            for n, (dz, dy) in enumerate(GX_OFFSETS):
                moves[h, n].wait_recv()
                if STOP >= 2:
                    convert(h, gx_peer((4 - dz) % 4, (4 - dy) % 4))
        if STOP >= 3:
            for first, at in ((0, 0), (2, 256)):
                rows, cols = pl.ds(at, 512 - at), pl.ds(at, 256)
                term = dot3((high[h, rows, :], low[h, rows, :]), (high[h, cols, :], low[h, cols, :]), (1, 1))
                for n, (i, j) in enumerate(BLOCKS):
                    if j in (first, first + 1):
                        block = term[i * 128 - at : i * 128 - at + 128, (j - first) * 128 : (j - first) * 128 + 128]
                        if h:
                            block = block + partial[pl.ds(n * 128, 128), :]
                        partial[pl.ds(n * 128, 128), :] = block

    size = SLICE * 8
    half = 16 * size
    me = x * 4 + y
    swaps, outs, passes, gathers, onward = {}, {}, {}, {}, {}
    halves = partial.reshape(32, size, 128)
    for p, (at, rows) in enumerate(PARTS):
        piece = pl.ds(at, rows)
        swaps[p] = remote(halves.at[rows_of(1 - c, 16), piece, :], core_buf.at[:, piece, :], csend.at[p], crecv.at[p], core_peer())
        swaps[p].start()
    for p, (at, rows) in enumerate(PARTS):
        piece = pl.ds(at, rows)
        swaps[p].wait_recv()
        part[:, piece, :] = halves[rows_of(c, 16), piece, :] + core_buf[:, piece, :]
        for n, (dx, dy) in enumerate(XY_OFFSETS):
            q, device = xy_peer(dx, dy)
            outs[p, n] = remote(part.at[q, piece], xy_buf.at[me, piece], xsend.at[p * 15 + n], xrecv.at[p * 15 + n], device)
            outs[p, n].start()
        xy_buf[me, piece, :] = part[me, piece, :]
    for p, (at, rows) in enumerate(PARTS):
        for n in range(15):
            outs[p, n].wait_recv()
        total = xy_buf[0, pl.ds(at, rows), :]
        for q in range(1, 16):
            total = total + xy_buf[q, pl.ds(at, rows), :]
        z_buf[z, pl.ds(at, rows), :] = total
        z_own[pl.ds(at, rows), :] = total
        for n, dz in enumerate(Z_OFFSETS):
            passes[p, n] = remote(z_own.at[pl.ds(at, rows)], z_buf.at[z, pl.ds(at, rows)], zsend.at[p * 7 + n], zrecv.at[p * 7 + n], z_peer(dz))
            passes[p, n].start()

    def slot(q, p):
        at, rows = PARTS[p]
        return done.at[pl.ds(pl.multiple_of(c * half + q * size + at, 8), rows)]

    for p, (at, rows) in enumerate(PARTS):
        for n in range(7):
            passes[p, n].wait_recv()
        total = z_buf[0, pl.ds(at, rows), :]
        for q in range(1, 8):
            total = total + z_buf[q, pl.ds(at, rows), :]
        done[pl.ds(pl.multiple_of(c * half + me * size + at, 8), rows), :] = total
        for n, (dx, dy) in enumerate(XY_OFFSETS):
            gathers[p, n] = remote(slot(me, p), slot(me, p), gsend.at[p * 15 + n], grecv.at[p * 15 + n], xy_peer(dx, dy)[1])
            gathers[p, n].start()
    near = [(0, 0)] + [XY_OFFSETS[n] for n in range(14, -1, -1)]
    for p in range(len(PARTS)):
        for n, (dx, dy) in enumerate(near):
            if n:
                gathers[p, 15 - n].wait_recv()
            q = lax.rem(x - dx + 4, 4) * 4 + lax.rem(y - dy + 4, 4)
            onward[p, n] = remote(slot(q, p), slot(q, p), fsend.at[p * 16 + n], frecv.at[p * 16 + n], core_peer())
            onward[p, n].start()

    def assemble(first):
        for n, (i, j) in enumerate(BLOCKS):
            if n // 5 == first:
                block = done[pl.ds(n * 128, 128), :]
                gram[pl.ds(i * 128, 128), pl.ds(j * 128, 128)] = block
                if i != j:
                    gram[pl.ds(j * 128, 128), pl.ds(i * 128, 128)] = block.T

    for first in range(2):
        pl.when(c == first)(functools.partial(assemble, first))
    for move in onward.values():
        move.wait_recv()
    for first in range(2):
        pl.when(c != first)(functools.partial(assemble, first))
    sent += [*swaps.values(), *outs.values(), *passes.values(), *gathers.values(), *onward.values()]

    if STOP >= 8:
        staged = stage.reshape(2 * 128 * 8, 128)
        backs = []

        def cells_at(h):
            return pl.ds(pl.multiple_of(gx % 2 * 16 + h * 8, 8), 8)

        def back(h, home, n, m):
            backs.append(remote(stage.at[h, rows_of(home, 8)], core.at[:, gx // 2, cells_at(h), :], bsend.at[n], brecv.at[m], (home, gy)))
            backs[-1].start()

        def ranks_done(r):
            ranks = pl.ds(32 * r, 32)
            rows = dot(inverse[ranks, :], image[...], (1, 0), HIGHEST)
            turned[ranks, :] = rows
            weights = split(rows)
            for h in range(2):
                block = dot3(weights, (high[h], low[h]), (1, 0))
                for b in range(8):
                    staged[pl.ds(h * 1024 + r * 256 + b, 32, stride=8), :] = block[:, b * 128 : b * 128 + 128]
                for dy in (2, 1, 3):
                    back(h, r * 4 + lax.rem(y + dy, 4), 6 + (h * 4 + r) * 3 + dy - 1, 6 + (h * 4 + zh) * 3 + dy - 1)

        image[...] = dot(turned[...], gram[...], (1, 0), HIGHEST)
        for step in range(ITERS):
            small = dot(image[...], image[...], (1, 1), HIGHEST)
            if step < ITERS - 1:
                ahead = dot(image[...], gram[...], (1, 0), HIGHEST)
                triangular_inverse(small, inverse)
                image[...] = dot(inverse[...], ahead, (1, 0), HIGHEST)
            else:
                triangular_inverse(small, inverse, ranks_done)
        for h in range(2):
            for dz in (2, 1, 3):
                back(h, gx_peer(dz, 0), h * 3 + dz - 1, h * 3 + dz - 1)
        factor[...] = turned[...].T * math.sqrt(512)
        for h in range(2):
            core[:, gx // 2, cells_at(h), :] = stage[h, rows_of(gx, 8)]
        for move in backs[24:]:
            move.wait_recv()
        for h in range(2):
            for source_zh in range(4):
                for dy in range(1, 4):
                    m = 6 + (h * 4 + source_zh) * 3 + dy - 1
                    remote(stage.at[h, rows_of(gx, 8)], core.at[:, gx // 2, cells_at(h), :], bsend.at[m], brecv.at[m], (gx_peer(0, dy), gy)).wait_recv()
        sent += backs
    for move in sent:
        move.wait_send()


VMEM = pl.BlockSpec(memory_space=pltpu.VMEM)
ANY = pl.BlockSpec(memory_space=pl.ANY)
DMA = pltpu.SemaphoreType.DMA


def finish(factor_in, core_in, factor, core, sems):
    copies = [pltpu.make_async_copy(core_in, core, sems.at[0]), pltpu.make_async_copy(factor_in, factor, sems.at[1])]
    for copy in copies:
        copy.start()
    for copy in copies:
        copy.wait()


def on_device(snapshot, start_factor):
    size = SLICE * 8
    outs = (jax.ShapeDtypeStruct((512, 128), F32), jax.ShapeDtypeStruct((8, 8, 32, 128), F32))
    results = pl.pallas_call(
        kernel,
        out_shape=outs,
        in_specs=[ANY, ANY],
        out_specs=(VMEM, VMEM),
        scratch_shapes=[
            pltpu.VMEM((2, 512, 8, 128), F32),
            pltpu.VMEM((2, 512, 1024), BF16),
            pltpu.VMEM((2, 512, 1024), BF16),
            pltpu.VMEM((1280, 128), F32),
            pltpu.VMEM((16, size, 128), F32),
            pltpu.VMEM((16, size, 128), F32),
            pltpu.VMEM((16, size, 128), F32),
            pltpu.VMEM((size, 128), F32),
            pltpu.VMEM((8, size, 128), F32),
            pltpu.VMEM((1280, 128), F32),
            pltpu.VMEM((512, 512), F32),
            pltpu.VMEM((512, 128), F32),
            pltpu.VMEM((128, 512), F32),
            pltpu.VMEM((128, 512), F32),
            pltpu.VMEM((128, 128), F32),
            pltpu.VMEM((2, 128, 8, 128), F32),
            DMA((2,)), DMA((30,)), DMA((30,)), DMA((2,)), DMA((2,)), DMA((30,)), DMA((30,)),
            DMA((14,)), DMA((14,)), DMA((30,)), DMA((30,)), DMA((32,)), DMA((32,)),
            DMA((30,)), DMA((30,)), pltpu.SemaphoreType.REGULAR((3,)), DMA((1,)),
        ],
        compiler_params=pltpu.CompilerParams(collective_id=0, has_side_effects=True, vmem_limit_bytes=LIMIT),
        name="hosvd_mode",
    )(snapshot, start_factor)
    return pl.pallas_call(
        finish,
        out_shape=outs,
        in_specs=[ANY, ANY],
        out_specs=(ANY, ANY),
        scratch_shapes=[DMA((2,))],
        compiler_params=pltpu.CompilerParams(vmem_limit_bytes=2**20),
        name="finish",
    )(*results)


def solution(mesh):
    return jax.shard_map(
        on_device,
        mesh=mesh,
        in_specs=(P(None, "gx", "gy", None), P()),
        out_specs=(P(), P("gx", None, "gy", None)),
        check_vma=False,
    )
```
